32 devices in a mesh: dp: 4 (over x, core), enc: 8 (over z, y).
Axes of the slice: x: 2, y: 2, z: 4, core: 2. Of those that a mesh axis runs over, the one named last changes fastest.
Arguments:
- counts: int32 [4, 8], P('dp'), may hold values from 1 to 48, 192 in all within a row
- pixels: bfloat16 [4, 6144, 392], P('dp', 'enc'), may hold values from -6 to 6
- cotangent: bfloat16 [4, 3072, 1728], P('dp', 'enc'), may hold values from -0.078125 to 0.078125
Outputs:
- grad_patch: float32 [1728, 392], P('enc')
The draws below stay inside these ranges and needn't reach their ends.
Inputs may be any that keep to these rules, and one draw needn't show every extreme that they name: `counts`: each row of a group sums to exactly 192; in each row some device holds exactly 48 live blocks.
All inputs are finite; a program needn't handle non-finite values.
Results may differ from the reference program's by a relative error of at most 0.0003.
Values may be sent and summed in bfloat16 or wider, within the bound.
A program may use at most 64 MiB of HBM per device.

```python
import math
import jax
import jax.numpy as jnp
import numpy as np
from jax import lax

D = 1728
PIX = 392
BLK = 16
OWNED = 24
IN_ROWS = 6144
OWN_ROWS = 3072
N_DP = 4
N_ENC = 8


def raised(values, key, source, target, blocks, factor):
    def block_of(axis_at):
        return (jnp.arange(values.shape[axis_at]) // (values.shape[axis_at] // blocks)).reshape((-1,) + (1,) * (values.ndim - 1 - axis_at))

    one_side = jax.random.permutation(key, blocks)[block_of(target)]
    far = (block_of(target) + blocks // 2) % blocks
    return jnp.where((block_of(source) == one_side) | (block_of(source) == far), factor * values, values)


def steps_of(key, extent, cuts, low, high):
    gain, own = 1.0, jax.random.fold_in(key, 6)
    for position, shards_of in cuts:
        draws = jnp.exp(jax.random.uniform(jax.random.fold_in(own, position), (shards_of,), jnp.float32, low / len(cuts), high / len(cuts)))
        gain = gain * jnp.repeat(draws, extent[position] // shards_of).reshape([-1 if axis == position else 1 for axis in range(len(extent))])
    return gain


def split_up(count, total, most, skew):
    loads = [(1 << 20) // math.isqrt(rank ** skew) + 1 for rank in range(2, count + 1)]
    rest, holding = total - most - (count - 1), [1] * (count - 1)
    while rest > 0:
        candidates = [i for i in range(count - 1) if holding[i] < most]
        mass, left = sum([loads[i] for i in candidates]), rest
        for i in candidates:
            more = min(most - holding[i], max(1, left * loads[i] // mass), rest)
            holding[i] = holding[i] + more
            rest = rest - more
    return np.array([most] + holding)


def uneven(rng, number_of, total, most, skew):
    if number_of == 2:
        one = jax.random.randint(rng, (), max(1, total - most), min(most, total - 1) + 1)
        return jnp.stack([one, total - one])
    lengths = jnp.asarray(split_up(number_of, total, most, skew), jnp.int32)
    pairs = (number_of - 1) // 2
    giver, sink = lengths[1:1 + 2 * pairs:2], lengths[2:2 + 2 * pairs:2]
    room = jnp.minimum(giver - 1, most - sink)
    passed = jax.random.randint(jax.random.fold_in(rng, 1), (pairs,), 0, 1 << 20) % (room + 1)
    lengths = lengths.at[1:1 + 2 * pairs:2].set(giver - passed).at[2:2 + 2 * pairs:2].set(sink + passed)
    return lengths[jax.random.permutation(jax.random.fold_in(rng, 2), number_of)]


def normal_values(own_key, dims, spread, reach, split=(), held_as=jnp.bfloat16):
    array = jax.random.normal(own_key, dims, jnp.float32) * spread
    if len(split) > 0:
        array = steps_of(own_key, dims, split, -0.22, 0.18) * array
    return jnp.clip(array, min=-reach, max=reach).astype(held_as)


def gaussian_with(own_key, extent, width, most, cuts, heavy, kind=jnp.bfloat16):
    array = width * jax.random.normal(own_key, extent, jnp.float32)
    if cuts:
        array = array * steps_of(own_key, extent, cuts, -0.22, 0.18)
    return jnp.clip(raised(array, jax.random.fold_in(own_key, 3), *heavy), -most, most).astype(kind)


def setup_inputs(seed: int = 0) -> dict:
    key_of = jax.random.split(jax.random.key(seed), 4)
    counts = jax.vmap(lambda own: uneven(own, N_ENC, OWNED * N_ENC, 2 * OWNED, 2))(jax.random.split(key_of[0], N_DP)).reshape((N_DP, N_ENC)).astype(jnp.int32)
    pixels = normal_values(key_of[1], (N_DP, IN_ROWS, PIX), 1.0, 6.0, ((0, 4), (1, 8)))
    cotangent = gaussian_with(key_of[2], (N_DP, OWN_ROWS, D), (N_DP * N_ENC * OWNED * BLK) ** -0.5, 0.078125, ((0, 4), (1, 8)), (1, 2, 8, 2.0))
    return dict(counts=counts, pixels=pixels, cotangent=cotangent)


def reference(counts, pixels, cotangent):
    n_enc = counts.shape[1]
    slots = 2 * OWNED

    def one_group(total, inputs):
        group_counts, group_pixels, group_cot = inputs
        ends = jnp.cumsum(group_counts).astype(jnp.int32)
        starts = (ends - group_counts).astype(jnp.int32)
        owner = jnp.arange(n_enc, dtype=jnp.int32)
        place = jnp.arange(OWNED, dtype=jnp.int32)
        global_ids = place[None, :] * n_enc + owner[:, None]
        anchor = jnp.sum((ends[None, None, :] <= global_ids[:, :, None]).astype(jnp.int32), axis=2).astype(jnp.int32)
        within = (global_ids - starts[anchor]).astype(jnp.int32)
        blocks = group_pixels.reshape(n_enc, slots, BLK, PIX)[anchor, within]
        rows = blocks.reshape(n_enc * OWNED * BLK, PIX)
        term = lax.dot_general(group_cot, rows, (((0,), (0,)), ((), ())), preferred_element_type=jnp.float32)
        return total + term, None

    total, _ = lax.scan(one_group, jnp.zeros((D, PIX), jnp.float32), (counts, pixels, cotangent))
    return total
```

```python
import functools
import jax
import jax.numpy as jnp
from jax import lax
from jax.experimental import pallas as pl
from jax.experimental.pallas import tpu as pltpu
from jax.sharding import PartitionSpec as P

BLK = 16
LANES = 128
MESH = pl.DeviceIdType.MESH


def lookup(table, index, peers):
    return jnp.sum(jnp.where(index[:, None] == peers[None, :], table[None, :], 0), axis=1)


def per_device(counts, pixels, cotangent):
    n_enc = lax.axis_size("enc")
    me_enc = lax.axis_index("enc")
    group_counts = counts[0]
    peers = jnp.arange(n_enc, dtype=jnp.int32)
    starts = jnp.sum(jnp.where(peers[None, :] < peers[:, None], group_counts[None, :], 0), axis=1)
    own_count = jnp.sum(jnp.where(peers == me_enc, group_counts, 0))
    own_start = jnp.sum(jnp.where(peers == me_enc, starts, 0))
    slots = pixels.shape[1] // BLK
    width = pixels.shape[2]
    per_peer = max(1, slots // n_enc)
    slot_ids = jnp.arange(slots, dtype=jnp.int32)
    global_ids = own_start + slot_ids
    target = global_ids % n_enc * per_peer + slot_ids // n_enc
    columns = jnp.arange(n_enc * per_peer, dtype=jnp.int32)
    select = (columns[:, None] == target[None, :]) & (slot_ids < own_count)[None, :]
    blocks = pixels[0].reshape(slots, BLK * width)
    outgoing = jnp.dot(
        select.astype(jnp.bfloat16), blocks, preferred_element_type=jnp.float32
    ).astype(jnp.bfloat16)
    arrived = lax.all_to_all(outgoing, "enc", split_axis=0, concat_axis=0, tiled=True)
    source = columns // per_peer
    rank = columns % per_peer
    src_start = lookup(starts, source, peers)
    src_count = lookup(group_counts, source, peers)
    first_slot = (me_enc - src_start) % n_enc
    slot_there = first_slot + rank * n_enc
    valid = slot_there < src_count
    compact = (src_start + slot_there) // n_enc
    own_blocks = cotangent.shape[1] // BLK
    compact_ids = jnp.arange(own_blocks, dtype=jnp.int32)
    order = (compact_ids[:, None] == compact[None, :]) & valid[None, :]
    owned = jnp.dot(order.astype(jnp.bfloat16), arrived, preferred_element_type=jnp.float32).astype(
        jnp.bfloat16
    )
    owned = owned.reshape(own_blocks * BLK, width)
    cot_rows = cotangent[0]
    local = lax.psum_scatter(
        lax.dot_general(
            cot_rows, owned, (((0,), (0,)), ((), ())), preferred_element_type=jnp.float32
        ),
        "enc",
        scatter_dimension=0,
        tiled=True,
    )
    return lax.psum(local, "dp")


def bits_of(number):
    return number.bit_length() - 1


def up(value, step):
    return -(-value // step) * step


def orders(ebits):
    near = [ebits, 0] + ([1] if ebits > 1 else [])
    far = list(range(2, ebits))
    return [near[i:] + near[:i] + far for i in range(len(near))]


def kernel(n_enc, plan, counts, pix, cot, out, *scratch):
    ebits = bits_of(n_enc)
    n_dp = 4
    per_peer = pix.shape[0]
    depth, own_rows = cot.shape
    rows = depth // n_enc
    half = up(up(rows, 2) // 2, 16)
    quarter = half // 2
    n_blocks = own_rows // BLK
    pieces = len(plan)
    it = iter(scratch)
    outgoing, arrived, owned, cot_other, part, place = (next(it) for _ in range(6))
    final, gathered = next(it), next(it)
    a2a_send, a2a_recv, core_send, core_recv, rs_send, rs_recv, dp_send, dp_recv = (next(it) for _ in range(8))
    work = [next(it) for _ in range(pieces)]
    landed, reduced = [], []
    for p in range(pieces):
        landed.append([next(it) for _ in range(ebits + 1)])
        reduced.append([next(it) for _ in range(ebits)])

    me = lax.axis_index("enc")
    dp = lax.axis_index("dp")
    core, x = lax.rem(dp, 2), dp // 2

    def enc_peer(j):
        peer = me
        for b in range(ebits):
            if (j >> b) & 1:
                peer = peer + (1 << b) - 2 * (1 << b) * lax.rem(me // (1 << b), 2)
        return peer

    def dp_peer(j):
        peer = dp
        for b in range(2):
            if (j >> b) & 1:
                peer = peer + (1 << b) - 2 * (1 << b) * lax.rem(dp // (1 << b), 2)
        return peer

    barrier = pltpu.get_barrier_semaphore()
    for j in range(1, n_enc):
        pl.semaphore_signal(barrier, inc=1, device_id=(dp, enc_peer(j)), device_id_type=MESH)
    for j in range(1, n_dp):
        pl.semaphore_signal(barrier, inc=1, device_id=(dp_peer(j), me), device_id_type=MESH)

    start = jnp.int32(0)
    for e in range(n_enc):
        start = start + jnp.where(e < me, counts[0, e], 0)
    start = lax.rem(start, n_enc)
    for d in range(n_enc):
        outgoing[d] = pix[:, lax.rem(d + n_enc - start, n_enc)]

    pl.semaphore_wait(barrier, n_enc + n_dp - 2)
    a2a = []
    for j in reversed(range(1, n_enc)):
        peer = enc_peer(j)
        copy = pltpu.make_async_remote_copy(
            src_ref=outgoing.at[peer],
            dst_ref=arrived.at[pl.ds(me * per_peer, per_peer)],
            send_sem=a2a_send.at[j - 1],
            recv_sem=a2a_recv.at[j - 1],
            device_id=(dp, peer),
            device_id_type=MESH,
        )
        copy.start()
        a2a.append(copy)

    core_cot = pltpu.make_async_remote_copy(
        src_ref=cot,
        dst_ref=cot_other,
        send_sem=core_send.at[0],
        recv_sem=core_recv.at[0],
        device_id=(dp_peer(1), me),
        device_id_type=MESH,
    )
    core_cot.start()

    def find(c, carry):
        g = c * n_enc + me
        source, first, end = jnp.int32(0), jnp.int32(0), jnp.int32(0)
        for e in range(n_enc):
            end = end + counts[0, e]
            past = end <= g
            source = source + jnp.where(past, 1, 0)
            first = jnp.where(past, end, first)
        place[c] = jnp.minimum(source * per_peer + (g - first) // n_enc, n_enc * per_peer - 1)
        return carry

    lax.fori_loop(0, n_blocks, find, 0)
    arrived[pl.ds(me * per_peer, per_peer)] = outgoing[me]
    for copy in a2a:
        copy.wait_recv()
    for c in range(n_blocks):
        owned[c * BLK : (c + 1) * BLK, :] = arrived[place[c]]
    core_pix = pltpu.make_async_remote_copy(
        src_ref=owned.at[pl.ds(0, own_rows)],
        dst_ref=owned.at[pl.ds(own_rows, own_rows)],
        send_sem=core_send.at[1],
        recv_sem=core_recv.at[1],
        device_id=(dp_peer(1), me),
        device_id_type=MESH,
    )
    core_pix.start()
    core_cot.wait_recv()
    core_pix.wait_recv()

    base = core * (rows - half)
    for i in range(n_enc // 2):
        these = slice(2 * rows * i, 2 * rows * (i + 1))
        part[...] = jnp.dot(
            cot[these, :], owned[:own_rows, :], preferred_element_type=jnp.float32
        ) + jnp.dot(cot_other[these, :], owned[own_rows:, :], preferred_element_type=jnp.float32)
        for j in range(2):
            e = 2 * i + j
            index = tuple((e >> b) & 1 for b in reversed(range(ebits)))
            for h in range(2):
                at = pl.ds(pl.multiple_of(rows * j + base + quarter * h, 8), quarter)
                for p, (low, wide, _) in enumerate(plan):
                    work[p][index + (h,)] = part[at, low : low + wide]

    def axis_of(a):
        if a == ebits:
            return x, (dp_peer(2), me)
        return lax.rem(me // (1 << a), 2), (dp, enc_peer(1 << a))

    held = list(work)
    left = [list(reversed(range(ebits))) + [ebits] for _ in range(pieces)]
    copies = [[] for _ in range(pieces)]

    def send(p, s):
        a = plan[p][2][s]
        mine, other = axis_of(a)
        ahead = (slice(None),) * left[p].index(a)
        copy = pltpu.make_async_remote_copy(
            src_ref=held[p].at[ahead + (1 - mine,)],
            dst_ref=landed[p][s],
            send_sem=rs_send.at[p, s],
            recv_sem=rs_recv.at[p, s],
            device_id=other,
            device_id_type=MESH,
        )
        copy.start()
        copies[p].append(copy)

    for p in range(pieces):
        send(p, 0)
    for s in range(ebits + 1):
        for p in range(pieces):
            low, wide, order = plan[p]
            a = order[s]
            mine, _ = axis_of(a)
            ahead = (slice(None),) * left[p].index(a)
            copies[p][s].wait_recv()
            total = held[p][ahead + (mine,)] + landed[p][s][...]
            if s < ebits:
                reduced[p][s][...] = total
                held[p] = reduced[p][s]
                left[p].remove(a)
                send(p, s + 1)
            else:
                final[:, low : low + wide] = total

    last = []
    for j in range(1, n_dp):
        copy = pltpu.make_async_remote_copy(
            src_ref=final,
            dst_ref=gathered.at[dp],
            send_sem=dp_send.at[j - 1],
            recv_sem=dp_recv.at[j - 1],
            device_id=(dp_peer(j), me),
            device_id_type=MESH,
        )
        copy.start()
        last.append(copy)
    gathered[dp] = final[...]
    for copy in last:
        copy.wait_recv()
    for d in range(n_dp):
        first = (d % 2) * (rows - half) + (d // 2) * quarter
        out[first : first + quarter, :] = gathered[d]
    for copy in a2a + [core_cot, core_pix] + sum(copies, []) + last:
        copy.wait_send()


def per_device_fused(n_enc, counts, pixels, cotangent):
    ebits = bits_of(n_enc)
    own_rows, depth = cotangent.shape[1:]
    width = pixels.shape[2]
    rows = depth // n_enc
    half = up(up(rows, 2) // 2, 16)
    quarter = half // 2
    slots = pixels.shape[1] // BLK
    per_peer = slots // n_enc
    turns = orders(ebits)
    plan = [
        (low, min(LANES, width - low), turns[i % len(turns)]) for i, low in enumerate(range(0, width, LANES))
    ]
    f32, bf16 = jnp.float32, jnp.bfloat16
    shapes = [
        pltpu.VMEM((n_enc, per_peer, BLK, width), bf16),
        pltpu.VMEM((slots, BLK, width), bf16),
        pltpu.VMEM((2 * own_rows, width), bf16),
        pltpu.VMEM((depth, own_rows), bf16),
        pltpu.VMEM((2 * rows, width), f32),
        pltpu.SMEM((own_rows // BLK,), jnp.int32),
        pltpu.VMEM((quarter, width), f32),
        pltpu.VMEM((4, quarter, width), f32),
        pltpu.SemaphoreType.DMA((n_enc - 1,)),
        pltpu.SemaphoreType.DMA((n_enc - 1,)),
        pltpu.SemaphoreType.DMA((2,)),
        pltpu.SemaphoreType.DMA((2,)),
        pltpu.SemaphoreType.DMA((len(plan), ebits + 1)),
        pltpu.SemaphoreType.DMA((len(plan), ebits + 1)),
        pltpu.SemaphoreType.DMA((3,)),
        pltpu.SemaphoreType.DMA((3,)),
    ]
    shapes += [pltpu.VMEM((2,) * (ebits + 1) + (quarter, wide), f32) for _, wide, _ in plan]
    for _, wide, _ in plan:
        shapes += [pltpu.VMEM((2,) * (ebits - s) + (quarter, wide), f32) for s in range(ebits + 1)]
        shapes += [pltpu.VMEM((2,) * (ebits - s) + (quarter, wide), f32) for s in range(ebits)]
    return pl.pallas_call(
        functools.partial(kernel, n_enc, plan),
        out_shape=jax.ShapeDtypeStruct((rows, width), f32),
        in_specs=[
            pl.BlockSpec(memory_space=pltpu.SMEM),
            pl.BlockSpec(memory_space=pltpu.VMEM),
            pl.BlockSpec(memory_space=pltpu.VMEM),
        ],
        out_specs=pl.BlockSpec(memory_space=pltpu.VMEM),
        scratch_shapes=shapes,
        compiler_params=pltpu.CompilerParams(
            collective_id=0, has_side_effects=True, vmem_limit_bytes=48 * 1024 * 1024
        ),
    )(counts, pixels[0].reshape(per_peer, n_enc, BLK, width), cotangent[0].T)


def fits(mesh, shapes):
    n_enc, n_dp = mesh.shape["enc"], mesh.shape["dp"]
    pixels, cotangent = shapes
    slots, own_rows, depth = pixels[1] // n_enc // BLK, cotangent[1] // n_enc, cotangent[2]
    return (
        n_dp == 1 << 2
        and n_enc > 1
        and n_enc == 1 << bits_of(n_enc)
        and slots % n_enc == 0
        and own_rows % LANES == 0
        and depth % (8 * n_enc) == 0
        and depth * pixels[2] * 4 < 4 * 1024 * 1024
    )


def solution(mesh):
    placed = (P("dp", None), P("dp", "enc", None), P("dp", "enc", None))

    def run(counts, pixels, cotangent):
        fused = fits(mesh, (pixels.shape, cotangent.shape))
        body = functools.partial(per_device_fused, mesh.shape["enc"]) if fused else per_device
        return jax.shard_map(
            body, mesh=mesh, in_specs=placed, out_specs=P("enc", None), check_vma=False
        )(counts, pixels, cotangent)

    return run
```

```python
import functools
import jax
import jax.numpy as jnp
from jax import lax
from jax.experimental import pallas as pl
from jax.experimental.pallas import tpu as pltpu
from jax.sharding import PartitionSpec as P

BLK = 16
LANES = 128
MESH = pl.DeviceIdType.MESH


def lookup(table, index, peers):
    return jnp.sum(jnp.where(index[:, None] == peers[None, :], table[None, :], 0), axis=1)


def per_device(counts, pixels, cotangent):
    n_enc = lax.axis_size("enc")
    me_enc = lax.axis_index("enc")
    group_counts = counts[0]
    peers = jnp.arange(n_enc, dtype=jnp.int32)
    starts = jnp.sum(jnp.where(peers[None, :] < peers[:, None], group_counts[None, :], 0), axis=1)
    own_count = jnp.sum(jnp.where(peers == me_enc, group_counts, 0))
    own_start = jnp.sum(jnp.where(peers == me_enc, starts, 0))
    slots = pixels.shape[1] // BLK
    width = pixels.shape[2]
    per_peer = max(1, slots // n_enc)
    slot_ids = jnp.arange(slots, dtype=jnp.int32)
    global_ids = own_start + slot_ids
    target = global_ids % n_enc * per_peer + slot_ids // n_enc
    columns = jnp.arange(n_enc * per_peer, dtype=jnp.int32)
    select = (columns[:, None] == target[None, :]) & (slot_ids < own_count)[None, :]
    blocks = pixels[0].reshape(slots, BLK * width)
    outgoing = jnp.dot(
        select.astype(jnp.bfloat16), blocks, preferred_element_type=jnp.float32
    ).astype(jnp.bfloat16)
    arrived = lax.all_to_all(outgoing, "enc", split_axis=0, concat_axis=0, tiled=True)
    source = columns // per_peer
    rank = columns % per_peer
    src_start = lookup(starts, source, peers)
    src_count = lookup(group_counts, source, peers)
    first_slot = (me_enc - src_start) % n_enc
    slot_there = first_slot + rank * n_enc
    valid = slot_there < src_count
    compact = (src_start + slot_there) // n_enc
    own_blocks = cotangent.shape[1] // BLK
    compact_ids = jnp.arange(own_blocks, dtype=jnp.int32)
    order = (compact_ids[:, None] == compact[None, :]) & valid[None, :]
    owned = jnp.dot(order.astype(jnp.bfloat16), arrived, preferred_element_type=jnp.float32).astype(
        jnp.bfloat16
    )
    owned = owned.reshape(own_blocks * BLK, width)
    cot_rows = cotangent[0]
    local = lax.psum_scatter(
        lax.dot_general(
            cot_rows, owned, (((0,), (0,)), ((), ())), preferred_element_type=jnp.float32
        ),
        "enc",
        scatter_dimension=0,
        tiled=True,
    )
    return lax.psum(local, "dp")


def bits_of(number):
    return number.bit_length() - 1


def up(value, step):
    return -(-value // step) * step


def orders(ebits, pieces):
    return [[ebits] + list(range(ebits)) for _ in range(pieces)]


def sizes(n_enc, slots, own_rows, depth, width):
    rows = depth // n_enc
    half = up(up(rows, 2) // 2, 16)
    pieces = width // LANES
    return rows, half, half // 2, slots // n_enc, pieces, width % LANES


def kernel(n_enc, counts, pix, cot, out, *scratch):
    ebits = bits_of(n_enc)
    n_dp = 4
    depth, own_rows = cot.shape
    rows, half, quarter, per_peer, pieces, tail = sizes(n_enc, pix.shape[0] * n_enc, own_rows, depth, pix.shape[3])
    low_tail = pieces * LANES
    stages = ebits + 1
    plan = orders(ebits, pieces)
    n_blocks = own_rows // BLK
    it = iter(scratch)
    cot_other, source_of, slot_of, tails = (next(it) for _ in range(4))
    a2a_send, a2a_recv, cot_send, cot_recv, pix_send, pix_recv, rs_send, rs_recv, dp_send, dp_recv = (
        next(it) for _ in range(10)
    )
    outgoing, arrived, owned, part, work, final, gathered = ([next(it) for _ in range(pieces)] for _ in range(7))
    landed = [[next(it) for _ in range(stages)] for _ in range(pieces)]
    reduced = [[next(it) for _ in range(ebits)] for _ in range(pieces)]
    chunk = [ref.shape[0] // n_enc for ref in arrived]

    me = lax.axis_index("enc")
    dp = lax.axis_index("dp")
    core, x = lax.rem(dp, 2), dp // 2

    def flipped(index, j, bits):
        for b in range(bits):
            if (j >> b) & 1:
                index = index + (1 << b) - 2 * (1 << b) * lax.rem(index // (1 << b), 2)
        return index

    def enc_peer(j):
        return flipped(me, j, ebits)

    def dp_peer(j):
        return flipped(dp, j, 2)

    def remote(src, dst, send_sem, recv_sem, device):
        copy = pltpu.make_async_remote_copy(
            src_ref=src, dst_ref=dst, send_sem=send_sem, recv_sem=recv_sem, device_id=device, device_id_type=MESH
        )
        copy.start()
        started.append(copy)
        return copy

    started = []
    barrier = pltpu.get_barrier_semaphore()
    for j in range(1, n_enc):
        pl.semaphore_signal(barrier, inc=1, device_id=(dp, enc_peer(j)), device_id_type=MESH)
    for j in range(1, n_dp):
        pl.semaphore_signal(barrier, inc=1, device_id=(dp_peer(j), me), device_id_type=MESH)

    start = jnp.int32(0)
    for e in range(n_enc):
        start = start + jnp.where(e < me, counts[0, e], 0)
    start = lax.rem(start, n_enc)

    def fill(p):
        for d in range(n_enc):
            r = lax.rem(d + n_enc - start, n_enc)
            outgoing[p][d * chunk[p] : d * chunk[p] + per_peer] = pix[:, r, :, p * LANES : (p + 1) * LANES]
            if p == 0:
                for k in range(per_peer):
                    outgoing[p][d * chunk[p] + per_peer, :, k * tail : (k + 1) * tail] = pix[k, r, :, low_tail:]

    a2a = [[] for _ in range(pieces)]

    def deal(p):
        for j in reversed(range(1, n_enc)):
            peer = enc_peer(j)
            a2a[p].append(
                remote(
                    outgoing[p].at[pl.ds(peer * chunk[p], chunk[p])],
                    arrived[p].at[pl.ds(me * chunk[p], chunk[p])],
                    a2a_send.at[p, j - 1],
                    a2a_recv.at[p, j - 1],
                    (dp, peer),
                )
            )

    fill(0)
    pl.semaphore_wait(barrier, n_enc + n_dp - 2)
    deal(0)
    core_cot = remote(cot, cot_other, cot_send.at[0], cot_recv.at[0], (dp_peer(1), me))
    for p in range(1, pieces):
        fill(p)
        deal(p)

    def find(c, carry):
        g = c * n_enc + me
        source, first, end = jnp.int32(0), jnp.int32(0), jnp.int32(0)
        for e in range(n_enc):
            end = end + counts[0, e]
            past = end <= g
            source = source + jnp.where(past, 1, 0)
            first = jnp.where(past, end, first)
        source_of[c] = jnp.minimum(source, n_enc - 1)
        slot_of[c] = jnp.minimum((g - first) // n_enc, per_peer - 1)
        return carry

    lax.fori_loop(0, n_blocks, find, 0)
    base = core * (rows - half)

    def axis_of(a):
        if a == ebits:
            return x, (dp_peer(2), me)
        return lax.rem(me // (1 << a), 2), (dp, enc_peer(1 << a))

    held = list(work)
    left = [list(reversed(range(ebits))) + [ebits] for _ in range(pieces)]
    copies = [[] for _ in range(pieces)]
    last = [[] for _ in range(pieces)]

    def send(p, s):
        a = plan[p][s]
        mine, other = axis_of(a)
        ahead = (slice(None),) * left[p].index(a)
        copies[p].append(
            remote(held[p].at[ahead + (1 - mine,)], landed[p][s], rs_send.at[p, s], rs_recv.at[p, s], other)
        )

    def launch(p):
        here = pl.ds(me * chunk[p], chunk[p])
        arrived[p][here] = outgoing[p][here]
        for copy in a2a[p]:
            copy.wait_recv()
        if p == 0:
            for e in range(n_enc):
                for k in range(per_peer):
                    tails[e * per_peer + k] = arrived[p][e * chunk[p] + per_peer, :, k * tail : (k + 1) * tail]
        for c in range(n_blocks):
            these = slice(c * BLK, (c + 1) * BLK)
            owned[p][these, :LANES] = arrived[p][source_of[c] * chunk[p] + slot_of[c]]
            if p == 0:
                owned[p][these, LANES:] = tails[source_of[c] * per_peer + slot_of[c]]
        swap = remote(
            owned[p].at[pl.ds(0, own_rows)],
            owned[p].at[pl.ds(own_rows, own_rows)],
            pix_send.at[p],
            pix_recv.at[p],
            (dp_peer(1), me),
        )
        if p == 0:
            core_cot.wait_recv()
        swap.wait_recv()
        for i in range(n_enc // 2):
            these = slice(2 * rows * i, 2 * rows * (i + 1))
            part[p][...] = jnp.dot(
                cot[these, :], owned[p][:own_rows, :], preferred_element_type=jnp.float32
            ) + jnp.dot(cot_other[these, :], owned[p][own_rows:, :], preferred_element_type=jnp.float32)
            for j in range(2):
                e = 2 * i + j
                index = tuple((e >> b) & 1 for b in reversed(range(ebits)))
                for h in range(2):
                    at = rows * j + base + quarter * h
                    work[p][index + (h, slice(0, quarter))] = part[p][pl.ds(pl.multiple_of(at, 8), quarter), :LANES]
                    if p == 0:
                        for r in range(quarter // 8):
                            work[p][index + (h, slice(quarter, quarter + 8), slice(r * tail, (r + 1) * tail))] = part[p][
                                pl.ds(pl.multiple_of(at + 8 * r, 8), 8), LANES:
                            ]
        send(p, 0)

    def advance(p, s):
        a = plan[p][s]
        mine, _ = axis_of(a)
        ahead = (slice(None),) * left[p].index(a)
        copies[p][s].wait_recv()
        total = held[p][ahead + (mine,)] + landed[p][s][...]
        if s < ebits:
            reduced[p][s][...] = total
            held[p] = reduced[p][s]
            left[p].remove(a)
            send(p, s + 1)
            return
        final[p][...] = total
        for j in range(1, n_dp):
            last[p].append(
                remote(final[p], gathered[p].at[dp], dp_send.at[p, j - 1], dp_recv.at[p, j - 1], (dp_peer(j), me))
            )
        gathered[p][dp] = total

    for tick in range(pieces + stages):
        if tick < pieces:
            launch(tick)
        for p in range(pieces):
            s = tick - p - 1
            if 0 <= s < stages:
                advance(p, s)
    for p in range(pieces):
        for copy in last[p]:
            copy.wait_recv()
        for d in range(n_dp):
            first = (d % 2) * (rows - half) + (d // 2) * quarter
            out[first : first + quarter, p * LANES : (p + 1) * LANES] = gathered[p][d, :quarter]
            if p == 0:
                for r in range(quarter // 8):
                    out[first + 8 * r : first + 8 * r + 8, low_tail:] = gathered[p][
                        d, quarter : quarter + 8, r * tail : (r + 1) * tail
                    ]
    for copy in started:
        copy.wait_send()


def per_device_fused(n_enc, counts, pixels, cotangent):
    ebits = bits_of(n_enc)
    own_rows, depth = cotangent.shape[1:]
    width = pixels.shape[2]
    slots = pixels.shape[1] // BLK
    rows, half, quarter, per_peer, pieces, tail = sizes(n_enc, slots, own_rows, depth, width)
    f32, bf16, dma = jnp.float32, jnp.bfloat16, pltpu.SemaphoreType.DMA
    stages = ebits + 1
    each = range(pieces)
    chunk = [per_peer + (p == 0) for p in each]
    wide = [LANES + tail * (p == 0) for p in each]
    tall = [quarter + 8 * (p == 0) for p in each]
    shapes = [
        pltpu.VMEM((depth, own_rows), bf16),
        pltpu.SMEM((own_rows // BLK,), jnp.int32),
        pltpu.SMEM((own_rows // BLK,), jnp.int32),
        pltpu.VMEM((slots, BLK, tail), bf16),
    ]
    for shape in ((pieces, n_enc - 1), (1,), (pieces,), (pieces, stages), (pieces, 3)):
        shapes += [dma(shape), dma(shape)]
    for _ in range(2):
        shapes += [pltpu.VMEM((n_enc * chunk[p], BLK, LANES), bf16) for p in each]
    shapes += [pltpu.VMEM((2 * own_rows, wide[p]), bf16) for p in each]
    shapes += [pltpu.VMEM((2 * rows, wide[p]), f32) for p in each]
    shapes += [pltpu.VMEM((2,) * stages + (tall[p], LANES), f32) for p in each]
    shapes += [pltpu.VMEM((tall[p], LANES), f32) for p in each]
    shapes += [pltpu.VMEM((4, tall[p], LANES), f32) for p in each]
    for p in each:
        shapes += [pltpu.VMEM((2,) * (ebits - s) + (tall[p], LANES), f32) for s in range(stages)]
    for p in each:
        shapes += [pltpu.VMEM((2,) * (ebits - s) + (tall[p], LANES), f32) for s in range(ebits)]
    return pl.pallas_call(
        functools.partial(kernel, n_enc),
        out_shape=jax.ShapeDtypeStruct((rows, width), f32),
        in_specs=[
            pl.BlockSpec(memory_space=pltpu.SMEM),
            pl.BlockSpec(memory_space=pltpu.VMEM),
            pl.BlockSpec(memory_space=pltpu.VMEM),
        ],
        out_specs=pl.BlockSpec(memory_space=pltpu.VMEM),
        scratch_shapes=shapes,
        compiler_params=pltpu.CompilerParams(
            collective_id=0, has_side_effects=True, vmem_limit_bytes=48 * 1024 * 1024
        ),
    )(counts, pixels[0].reshape(per_peer, n_enc, BLK, width), cotangent[0].T)


def fits(mesh, shapes):
    n_enc, n_dp = mesh.shape["enc"], mesh.shape["dp"]
    pixels, cotangent = shapes
    slots, own_rows, depth = pixels[1] // n_enc // BLK, cotangent[1] // n_enc, cotangent[2]
    return (
        n_dp == 1 << 2
        and n_enc > 1
        and n_enc == 1 << bits_of(n_enc)
        and slots % n_enc == 0
        and own_rows % LANES == 0
        and depth % (8 * n_enc) == 0
        and pixels[2] >= LANES
        and 0 < pixels[2] % LANES * max(slots // n_enc, depth // n_enc // 16) <= LANES
        and depth * pixels[2] * 4 < 4 * 1024 * 1024
    )


def solution(mesh):
    placed = (P("dp", None), P("dp", "enc", None), P("dp", "enc", None))

    def run(counts, pixels, cotangent):
        fused = fits(mesh, (pixels.shape, cotangent.shape))
        body = functools.partial(per_device_fused, mesh.shape["enc"]) if fused else per_device
        return jax.shard_map(
            body, mesh=mesh, in_specs=placed, out_specs=P("enc", None), check_vma=False
        )(counts, pixels, cotangent)

    return run
```
